512 devices in a mesh: ctx: 64 (over z_hi, y, x, core), head: 8 (over z_lo).
Axes of the slice: x: 4, y: 4, z: 16 (z_hi: 2, z_lo: 8; z = z_hi * 8 + z_lo), core: 2. Of those that a mesh axis runs over, the one named last changes fastest.
Arguments:
- queries: bfloat16 [32768, 5120], P(('ctx', 'head')), may hold values from -6 to 6
- keys: bfloat16 [32768, 5120], P(('ctx', 'head')), may hold values from -6 to 6
- values: bfloat16 [32768, 5120], P(('ctx', 'head')), may hold values from -6 to 6
- grad_out: bfloat16 [32768, 5120], P(('ctx', 'head')), may hold values from -150 to 150
- neighbours: int32 [512, 16], replicated, may hold values from 0 to 511, as said below
- counts: int32 [512], replicated, may hold values from 1 to 16, as said below
Outputs:
- grad_queries: bfloat16 [32768, 5120], P(('ctx', 'head'))
- grad_keys: bfloat16 [32768, 5120], P(('ctx', 'head'))
- grad_values: bfloat16 [32768, 5120], P(('ctx', 'head'))
The draws below stay inside these ranges and needn't reach their ends.
Inputs may be any that keep to these rules, and one draw needn't show every extreme that they name: `neighbours`: row t holds 16 distinct tile numbers; the first is t itself; each lies in t's slab of 8 tiles (tiles s * 8 to s * 8 + 7) or within the 8 tiles of the slabs beside it that are nearest to it. For the first tile of a slab that is not the first slab, the second entry is the tile just below it; for the last tile of a slab that is not the last slab, the second entry is the tile just above it. `counts`: the first tile of every slab uses all 16 entries; the last tile of every slab uses 2 or more.
All inputs are finite; a program needn't handle non-finite values.
Results may differ from the reference program's by a relative error of at most 0.0095.
Values may be sent and summed in bfloat16 or wider, within the bound.
A program may use at most 128 MiB of HBM per device.

```python
import math
import jax
import jax.numpy as jnp
from jax import lax

HEADS = 40
DH = 128
TILE = 64
HALO_TILES = 8
NBR = 16
TILES_DEV = 8
FEAT = 5120
TILES = 512
TOKENS = 32768


def draw_queries(key, part):
    key = jax.random.fold_in(key, 11)
    base = jnp.clip(jax.random.normal(key, (TOKENS, HEADS * DH), jnp.float32), -4.0, 4.0)
    return base.astype(jnp.bfloat16)


def draw_keys(key, part):
    key = jax.random.fold_in(key, 12)
    base = jnp.clip(jax.random.normal(key, (TOKENS, HEADS * DH), jnp.float32), -4.0, 4.0)
    return base.astype(jnp.bfloat16)


def draw_neighbours(key, part):
    key = jax.random.fold_in(key, 21)
    width = TILES_DEV + 2 * HALO_TILES
    tiles = jnp.arange(TILES, dtype=jnp.int32)
    slab_of = tiles // TILES_DEV
    offsets = jnp.arange(width, dtype=jnp.int32)
    candidate = slab_of[:, None] * TILES_DEV - HALO_TILES + offsets[None, :]
    inside = (candidate >= 0) & (candidate < TILES)
    distance = jnp.abs(candidate - tiles[:, None])
    crossing = candidate // TILES_DEV != slab_of[:, None]
    klass = jnp.where(distance == 0, 0, jnp.where((distance == 1) & crossing, 1, 2))
    klass = jnp.where(inside, klass, 3)
    noise = jax.random.randint(key, (TILES, width), 0, 4096, dtype=jnp.int32)
    score = klass * 1048576 + noise * 128 + offsets[None, :]
    order = jnp.argsort(score, axis=1)[:, :NBR]
    return jnp.take_along_axis(candidate, order, axis=1).astype(jnp.int32)


def draw_counts(key, part):
    key = jax.random.fold_in(key, 31)
    level_key, count_key, last_key = jax.random.split(key, 3)
    slab_total = TILES // TILES_DEV
    levels = jax.random.randint(level_key, (slab_total,), max(NBR // 4, 1), NBR + 1, dtype=jnp.int32)
    tiles = jnp.arange(TILES, dtype=jnp.int32)
    tile_level = levels[tiles // TILES_DEV]
    drawn = jax.random.randint(count_key, (TILES,), 1, tile_level + 1, dtype=jnp.int32)
    last_drawn = jax.random.randint(last_key, (TILES,), 2, NBR + 1, dtype=jnp.int32)
    inner = tiles % TILES_DEV
    result = jnp.where(inner == TILES_DEV - 1, last_drawn, drawn)
    return jnp.where(inner == 0, NBR, result).astype(jnp.int32)


def shard_levels(own_key, shape, cuts, least, high):
    def one(dim, parts):
        draws = jax.random.uniform(jax.random.fold_in(jax.random.fold_in(own_key, 6), dim), (parts,), jnp.float32, least / len(cuts), high / len(cuts))
        return jnp.repeat(jnp.exp(draws), shape[dim] // parts).reshape((-1,) + (1,) * (len(shape) - dim - 1))

    factor_of = one(*cuts[0])
    for cut in cuts[1:]:
        factor_of = factor_of * one(*cut)
    return factor_of


def scatter_about(key, shape, deviation, limit, cuts=(), held_as=jnp.bfloat16):
    values = jax.random.normal(key, shape, jnp.float32) * deviation
    if len(cuts) > 0:
        values = shard_levels(key, shape, cuts, -0.22, 0.18) * values
    return jnp.clip(values, min=-limit, max=limit).astype(held_as)


def setup_inputs(seed: int = 0) -> dict:
    splits = jax.random.split(jax.random.key(seed), 7)
    return {
        "queries": draw_queries(jax.random.fold_in(splits[6], 71), 0),
        "keys": draw_keys(jax.random.fold_in(splits[6], 71), 0),
        "values": scatter_about(splits[2], (TOKENS, FEAT), 1.0, 6.0, ((0, 512),)),
        "grad_out": scatter_about(splits[3], (TOKENS, FEAT), 30.0, 150.0, ((0, 512),)),
        "neighbours": draw_neighbours(jax.random.fold_in(splits[6], 71), 0),
        "counts": draw_counts(jax.random.fold_in(splits[6], 71), 0),
    }


def tile_mask(rows_nbr, rows_cnt, first_id, ncols):
    relative = rows_nbr - first_id
    listed = jnp.arange(rows_nbr.shape[1], dtype=jnp.int32)[None, :] < rows_cnt[:, None]
    columns = jnp.arange(ncols, dtype=jnp.int32)
    matched = (relative[:, :, None] == columns[None, None, :]) & listed[:, :, None]
    permitted = jnp.any(matched, axis=1)
    return jnp.repeat(jnp.repeat(permitted, TILE, axis=0), TILE, axis=1)

def reference(queries, keys, values, grad_out, neighbours, counts):
    row_count = TILES_DEV * TILE
    reach_rows = HALO_TILES * TILE
    window = row_count + 2 * reach_rows
    scale = 1.0 / math.sqrt(DH)
    padding = ((reach_rows, reach_rows), (0, 0))
    keys_pad = jnp.pad(keys, padding)
    values_pad = jnp.pad(values, padding)
    zeros = jnp.zeros((TOKENS + 2 * reach_rows, HEADS * DH), jnp.float32)

    def split_heads(array):
        return array.reshape(array.shape[0], HEADS, DH).astype(jnp.float32)

    def slab_step(carry, slab_index):
        grad_k, grad_v = carry
        start = (slab_index * row_count).astype(jnp.int32)
        tile_start = (slab_index * TILES_DEV).astype(jnp.int32)
        query_h = split_heads(lax.dynamic_slice_in_dim(queries, start, row_count, 0))
        cotan_h = split_heads(lax.dynamic_slice_in_dim(grad_out, start, row_count, 0))
        key_h = split_heads(lax.dynamic_slice_in_dim(keys_pad, start, window, 0))
        value_h = split_heads(lax.dynamic_slice_in_dim(values_pad, start, window, 0))
        slab_nbr = lax.dynamic_slice_in_dim(neighbours, tile_start, TILES_DEV, 0)
        slab_cnt = lax.dynamic_slice_in_dim(counts, tile_start, TILES_DEV, 0)
        permitted = tile_mask(slab_nbr, slab_cnt, tile_start - HALO_TILES, TILES_DEV + 2 * HALO_TILES)[None]
        scores = jnp.einsum('rhd,whd->hrw', query_h, key_h) * scale
        top_score = lax.optimization_barrier(jnp.max(jnp.where(permitted, scores, -jnp.inf), axis=2, keepdims=True))
        expo = jnp.where(permitted, jnp.exp(scores - top_score), 0.0)
        probs = expo / lax.optimization_barrier(jnp.sum(expo, axis=2, keepdims=True))
        probs_b = lax.optimization_barrier(probs.astype(jnp.bfloat16)).astype(jnp.float32)
        output = jnp.einsum('hrw,whd->hrd', probs_b, value_h)
        delta = lax.optimization_barrier(jnp.sum(jnp.transpose(cotan_h, (1, 0, 2)) * output, axis=2, keepdims=True))
        grad_p = jnp.einsum('rhd,whd->hrw', cotan_h, value_h)
        grad_s = probs * (grad_p - delta)
        grad_sb = lax.optimization_barrier(grad_s.astype(jnp.bfloat16)).astype(jnp.float32)
        grad_q = jnp.einsum('hrw,whd->rhd', grad_sb, key_h) * scale
        part_k = jnp.einsum('hrw,rhd->whd', grad_sb, query_h) * scale
        part_v = jnp.einsum('hrw,rhd->whd', probs_b, cotan_h)
        grad_k = lax.dynamic_update_slice_in_dim(grad_k, lax.dynamic_slice_in_dim(grad_k, start, window, 0) + part_k.reshape(window, HEADS * DH), start, 0)
        grad_v = lax.dynamic_update_slice_in_dim(grad_v, lax.dynamic_slice_in_dim(grad_v, start, window, 0) + part_v.reshape(window, HEADS * DH), start, 0)
        return ((grad_k, grad_v), grad_q.reshape(row_count, HEADS * DH).astype(jnp.bfloat16))
    slab_ids = jnp.arange(TILES // TILES_DEV, dtype=jnp.int32)
    (grad_k, grad_v), grad_q = lax.scan(slab_step, (zeros, zeros), slab_ids)
    grad_queries = grad_q.reshape(TOKENS, HEADS * DH)
    grad_keys = grad_k[reach_rows:reach_rows + TOKENS].astype(jnp.bfloat16)
    grad_values = grad_v[reach_rows:reach_rows + TOKENS].astype(jnp.bfloat16)
    return (grad_queries, grad_keys, grad_values)
```

```python
import functools
import math

import jax
import jax.numpy as jnp
from jax import lax
from jax.experimental import pallas as pl
from jax.experimental.pallas import tpu as pltpu
from jax.sharding import PartitionSpec as P

DH = 128
TILE = 64
MESH = pl.DeviceIdType.MESH
AHEAD = 2


def wait_bytes(ref, sem):
    pltpu.make_async_copy(ref, ref, sem).wait()


def kernel(
    slabs, width, head_count, block,
    q_in, k_in, v_in, d_in, listed,
    dq_out, dk_out, dv_out,
    q_rows, d_rows, k_win, v_win, bias, acc_k, acc_v, own, part_out, part_in, stage,
    in_send, in_recv, halo_send, halo_recv, part_send, part_recv, out_send, out_recv,
):
    slab = lax.axis_index("ctx")
    place = lax.axis_index("head")
    rows = width * TILE
    above, below = (slab + 1) % slabs, (slab + slabs - 1) % slabs

    def flipped(index):
        return index // (slabs // 2)

    def group_at(where):
        return where + flipped(slab) * (width - 1 - 2 * where)

    def beside(other):
        crossing = (flipped(slab) + flipped(other)) % 2
        return (other, place + crossing * (width - 1 - 2 * place))

    group = group_at(place)
    near = (beside(below), beside(above))
    steps = sorted(range(1, width), key=lambda j: (abs(j - width // 2), j))
    scale = 1.0 / math.sqrt(DH)

    barrier = pltpu.get_barrier_semaphore()
    for j in steps:
        pl.semaphore_signal(
            barrier, inc=1, device_id=(slab, (place + j) % width), device_id_type=MESH
        )
    for target in near:
        pl.semaphore_signal(barrier, inc=1, device_id=target, device_id_type=MESH)
    pl.semaphore_wait(barrier, width + 1)

    def head_columns(which, head):
        return pl.ds(pl.multiple_of((which * head_count + head) * DH, DH), DH)

    own_rows = pl.ds(rows + pl.multiple_of(place * TILE, TILE), TILE)
    slab_rows = pl.ds(pl.multiple_of(place * TILE, TILE), TILE)
    inputs = (
        (k_in, k_win, own_rows), (v_in, v_win, own_rows),
        (q_in, q_rows, slab_rows), (d_in, d_rows, slab_rows),
    )

    def send_inputs(head):
        for i, (source, target, where) in enumerate(inputs):
            for j in steps:
                other = (place + j) % width
                pltpu.make_async_remote_copy(
                    src_ref=source.at[:, head_columns(group_at(other), head)],
                    dst_ref=target.at[head, where],
                    send_sem=in_send.at[i],
                    recv_sem=in_recv.at[i, head],
                    device_id=(slab, other),
                    device_id_type=MESH,
                ).start()
            pltpu.make_async_copy(
                source.at[:, head_columns(group, head)],
                target.at[head, where],
                in_recv.at[i, head],
            ).start()

    def send_halo(head):
        for i, window in enumerate((k_win, v_win)):
            for side in range(2):
                pltpu.make_async_remote_copy(
                    src_ref=window.at[head, pl.ds(rows, rows)],
                    dst_ref=window.at[head, pl.ds(2 * rows * (1 - side), rows)],
                    send_sem=halo_send.at[i, side],
                    recv_sem=halo_recv.at[i, 1 - side, head],
                    device_id=near[side],
                    device_id_type=MESH,
                ).start()

    def send_result(index, head, target):
        for j in steps:
            other = (place + j) % width
            pltpu.make_async_remote_copy(
                src_ref=stage.at[index, head, pl.ds(pl.multiple_of(other * TILE, TILE), TILE)],
                dst_ref=target.at[:, head_columns(group, head)],
                send_sem=out_send.at[index],
                recv_sem=out_recv.at[index],
                device_id=(slab, other),
                device_id_type=MESH,
            ).start()
        pltpu.make_async_copy(
            stage.at[index, head, slab_rows],
            target.at[:, head_columns(group, head)],
            out_recv.at[index],
        ).start()

    def attend(head):
        acc_k[...] = jnp.zeros_like(acc_k)
        acc_v[...] = jnp.zeros_like(acc_v)

        @pl.loop(0, rows // block)
        def _(step):
            start = pl.multiple_of(step * block, block)
            picked = pl.ds(start, block)
            query, cotan = q_rows[head, picked], d_rows[head, picked]
            key, value = k_win[head], v_win[head]
            last = (((1,), (1,)), ((), ()))
            first = (((0,), (0,)), ((), ()))
            scores = lax.dot_general(key, query, last, preferred_element_type=jnp.float32)
            scores = scores.reshape(3 * width, TILE, block) * (scale / math.log(2.0))
            scores = (scores + bias[:, picked][:, None, :]).reshape(3 * rows, block)
            expo = jnp.exp2(scores - jnp.max(scores, axis=0, keepdims=True))
            probs = expo * (1.0 / jnp.sum(expo, axis=0, keepdims=True))
            grad_p = lax.dot_general(value, cotan, last, preferred_element_type=jnp.float32)
            delta = jnp.sum(probs * grad_p, axis=0, keepdims=True)
            grad_s = (probs * (grad_p - delta)).astype(jnp.bfloat16)
            acc_v[...] += jnp.dot(
                probs.astype(jnp.bfloat16), cotan, preferred_element_type=jnp.float32
            )
            acc_k[...] += jnp.dot(grad_s, query, preferred_element_type=jnp.float32)
            grad_q = lax.dot_general(grad_s, key, first, preferred_element_type=jnp.float32)
            stage[0, head, picked] = (grad_q * scale).astype(jnp.bfloat16)

        for i, (acc, factor) in enumerate(((acc_k, scale), (acc_v, 1.0))):
            own[i, head] = acc[rows : 2 * rows] * factor
            part_out[0, i, head] = (acc[:rows] * factor).astype(jnp.bfloat16)
            part_out[1, i, head] = (acc[2 * rows :] * factor).astype(jnp.bfloat16)

    def send_parts(head):
        for i in range(2):
            for side in range(2):
                pltpu.make_async_remote_copy(
                    src_ref=part_out.at[side, i, head],
                    dst_ref=part_in.at[1 - side, i, head],
                    send_sem=part_send.at[i, side],
                    recv_sem=part_recv.at[i, 1 - side, head],
                    device_id=near[side],
                    device_id_type=MESH,
                ).start()

    def finish(head):
        for i, target in enumerate((dk_out, dv_out)):
            for side in range(2):
                wait_bytes(part_in.at[side, i, head], part_recv.at[i, side, head])
            total = (
                own[i, head]
                + part_in[0, i, head].astype(jnp.float32)
                + part_in[1, i, head].astype(jnp.float32)
            )
            stage[1 + i, head] = total.astype(jnp.bfloat16)
            send_result(1 + i, head, target)

    for head in range(min(AHEAD, head_count)):
        send_inputs(head)

    tiles = lax.broadcasted_iota(jnp.int32, bias.shape, 0)
    hit = tiles == listed[0:1, :]
    for n in range(1, listed.shape[0]):
        hit = hit | (tiles == listed[n : n + 1, :])
    bias[...] = jnp.where(hit, 0.0, -1e30)

    @pl.loop(0, head_count)
    def _(head):
        for i, window in enumerate((k_win, v_win)):
            wait_bytes(window.at[head, pl.ds(rows, rows)], in_recv.at[i, head])
        send_halo(head)

        @pl.when(head + AHEAD < head_count)
        def _():
            send_inputs(head + AHEAD)

        wait_bytes(q_rows.at[head], in_recv.at[2, head])
        wait_bytes(d_rows.at[head], in_recv.at[3, head])
        for i, window in enumerate((k_win, v_win)):
            for side in range(2):
                wait_bytes(
                    window.at[head, pl.ds(2 * rows * side, rows)], halo_recv.at[i, side, head]
                )
        attend(head)
        send_parts(head)
        send_result(0, head, dq_out)

        @pl.when(head >= 1)
        def _():
            finish(head - 1)

    finish(head_count - 1)

    remote = pl.ds(0, rows - TILE)
    for i in range(4):
        wait_bytes(k_win.at[:, remote], in_send.at[i])
    for i in range(2):
        for side in range(2):
            wait_bytes(q_rows, halo_send.at[i, side])
            wait_bytes(q_rows, part_send.at[i, side])
    for i, target in enumerate((dq_out, dk_out, dv_out)):
        wait_bytes(stage.at[i, :, remote], out_send.at[i])
        wait_bytes(target, out_recv.at[i])


def per_device(slabs, width, queries, keys, values, grad_out, neighbours, counts):
    tile_rows, features = queries.shape
    head_count = features // DH // width
    rows = width * TILE
    first = lax.axis_index("ctx") * width
    own_nbr = lax.dynamic_slice_in_dim(neighbours, first, width, 0)
    own_cnt = lax.dynamic_slice_in_dim(counts, first, width, 0)
    used = lax.broadcasted_iota(jnp.int32, own_nbr.shape, 1) < own_cnt[:, None]
    listed = jnp.repeat(jnp.where(used, own_nbr - first + width, -1).T, TILE, axis=1)
    block = min(256, rows)
    whole = pl.BlockSpec(memory_space=pl.ANY)
    half = jnp.bfloat16
    dma = pltpu.SemaphoreType.DMA
    flops = 5 * 2 * rows * 3 * rows * DH * head_count
    return pl.pallas_call(
        functools.partial(kernel, slabs, width, head_count, block),
        out_shape=[jax.ShapeDtypeStruct((tile_rows, features), half)] * 3,
        in_specs=[whole] * 4 + [pl.BlockSpec(memory_space=pltpu.VMEM)],
        out_specs=[whole] * 3,
        scratch_shapes=[
            pltpu.VMEM((head_count, rows, DH), half),
            pltpu.VMEM((head_count, rows, DH), half),
            pltpu.VMEM((head_count, 3 * rows, DH), half),
            pltpu.VMEM((head_count, 3 * rows, DH), half),
            pltpu.VMEM((3 * width, rows), jnp.float32),
            pltpu.VMEM((3 * rows, DH), jnp.float32),
            pltpu.VMEM((3 * rows, DH), jnp.float32),
            pltpu.VMEM((2, head_count, rows, DH), jnp.float32),
            pltpu.VMEM((2, 2, head_count, rows, DH), half),
            pltpu.VMEM((2, 2, head_count, rows, DH), half),
            pltpu.VMEM((3, head_count, rows, DH), half),
            dma((4,)),
            dma((4, head_count)),
            dma((2, 2)),
            dma((2, 2, head_count)),
            dma((2, 2)),
            dma((2, 2, head_count)),
            dma((3,)),
            dma((3,)),
        ],
        compiler_params=pltpu.CompilerParams(
            collective_id=0, has_side_effects=True, vmem_limit_bytes=56 * 1024 * 1024
        ),
        cost_estimate=pl.CostEstimate(
            flops=flops, bytes_accessed=7 * tile_rows * features * 2, transcendentals=0
        ),
    )(queries, keys, values, grad_out, listed)


def solution(mesh):
    split = P(("ctx", "head"), None)
    return jax.shard_map(
        functools.partial(per_device, mesh.shape["ctx"], mesh.shape["head"]),
        mesh=mesh,
        in_specs=(split, split, split, split, P(), P()),
        out_specs=(split, split, split),
        check_vma=False,
    )
```

```python
import functools
import math

import jax
import jax.numpy as jnp
from jax import lax
from jax.experimental import pallas as pl
from jax.experimental.pallas import tpu as pltpu
from jax.sharding import PartitionSpec as P

DH = 128
TILE = 64
MESH = pl.DeviceIdType.MESH
AHEAD = 2


def wait_bytes(ref, sem):
    pltpu.make_async_copy(ref, ref, sem).wait()


def kernel(
    slabs, width, head_count, block,
    q_in, k_in, v_in, d_in, neighbours, counts,
    dq_out, dk_out, dv_out,
    q_rows, d_rows, k_win, v_win, listed, bias, acc_k, acc_v, own, part_out, part_in, stage, list_sem,
    in_send, in_recv, halo_send, halo_recv, part_send, part_recv, out_send, out_recv,
):
    slab = lax.axis_index("ctx")
    place = lax.axis_index("head")
    rows = width * TILE
    above, below = (slab + 1) % slabs, (slab + slabs - 1) % slabs

    def flipped(index):
        return index // (slabs // 2)

    def group_at(where):
        return where + flipped(slab) * (width - 1 - 2 * where)

    def beside(other):
        crossing = (flipped(slab) + flipped(other)) % 2
        return (other, place + crossing * (width - 1 - 2 * place))

    group = group_at(place)
    near = (beside(below), beside(above))
    steps = sorted(range(1, width), key=lambda j: (abs(j - width // 2), j))
    scale = 1.0 / math.sqrt(DH)

    lists = pltpu.make_async_copy(
        neighbours.at[pl.ds(pl.multiple_of(slab * width, width), width)], listed, list_sem
    )
    lists.start()

    barrier = pltpu.get_barrier_semaphore()
    for j in steps:
        pl.semaphore_signal(
            barrier, inc=1, device_id=(slab, (place + j) % width), device_id_type=MESH
        )
    for target in near:
        pl.semaphore_signal(barrier, inc=1, device_id=target, device_id_type=MESH)
    pl.semaphore_wait(barrier, width + 1)

    def head_columns(which, head):
        return pl.ds(pl.multiple_of((which * head_count + head) * DH, DH), DH)

    own_rows = pl.ds(rows + pl.multiple_of(place * TILE, TILE), TILE)
    slab_rows = pl.ds(pl.multiple_of(place * TILE, TILE), TILE)
    pair_kv = ((0, k_in, k_win, own_rows), (1, v_in, v_win, own_rows))
    pair_qd = ((2, q_in, q_rows, slab_rows), (3, d_in, d_rows, slab_rows))

    def send_inputs(pair, head):
        for i, source, target, where in pair:
            for j in steps:
                other = (place + j) % width
                pltpu.make_async_remote_copy(
                    src_ref=source.at[:, head_columns(group_at(other), head)],
                    dst_ref=target.at[head, where],
                    send_sem=in_send.at[i],
                    recv_sem=in_recv.at[i, head],
                    device_id=(slab, other),
                    device_id_type=MESH,
                ).start()
            pltpu.make_async_copy(
                source.at[:, head_columns(group, head)],
                target.at[head, where],
                in_recv.at[i, head],
            ).start()

    def send_halo(head):
        for i, window in enumerate((k_win, v_win)):
            for side in range(2):
                pltpu.make_async_remote_copy(
                    src_ref=window.at[head, pl.ds(rows, rows)],
                    dst_ref=window.at[head, pl.ds(2 * rows * (1 - side), rows)],
                    send_sem=halo_send.at[i, side],
                    recv_sem=halo_recv.at[i, 1 - side, head],
                    device_id=near[side],
                    device_id_type=MESH,
                ).start()

    def send_result(index, head, target):
        for j in steps:
            other = (place + j) % width
            pltpu.make_async_remote_copy(
                src_ref=stage.at[index, head, pl.ds(pl.multiple_of(other * TILE, TILE), TILE)],
                dst_ref=target.at[:, head_columns(group, head)],
                send_sem=out_send.at[index],
                recv_sem=out_recv.at[index],
                device_id=(slab, other),
                device_id_type=MESH,
            ).start()
        pltpu.make_async_copy(
            stage.at[index, head, slab_rows],
            target.at[:, head_columns(group, head)],
            out_recv.at[index],
        ).start()

    def attend(head):
        acc_k[...] = jnp.zeros_like(acc_k)
        acc_v[...] = jnp.zeros_like(acc_v)

        @pl.loop(0, rows // block)
        def _(step):
            start = pl.multiple_of(step * block, block)
            picked = pl.ds(start, block)
            query, cotan = q_rows[head, picked], d_rows[head, picked]
            key, value = k_win[head], v_win[head]
            last = (((1,), (1,)), ((), ()))
            first = (((0,), (0,)), ((), ()))
            scores = lax.dot_general(key, query, last, preferred_element_type=jnp.float32)
            scores = scores.reshape(3 * width, TILE, block) * (scale / math.log(2.0))
            scores = (scores + bias[:, picked][:, None, :]).reshape(3 * rows, block)
            expo = jnp.exp2(scores - jnp.max(scores, axis=0, keepdims=True))
            probs = expo * (1.0 / jnp.sum(expo, axis=0, keepdims=True))
            grad_p = lax.dot_general(value, cotan, last, preferred_element_type=jnp.float32)
            delta = jnp.sum(probs * grad_p, axis=0, keepdims=True)
            grad_s = (probs * (grad_p - delta)).astype(jnp.bfloat16)
            acc_v[...] += jnp.dot(
                probs.astype(jnp.bfloat16), cotan, preferred_element_type=jnp.float32
            )
            acc_k[...] += jnp.dot(grad_s, query, preferred_element_type=jnp.float32)
            grad_q = lax.dot_general(grad_s, key, first, preferred_element_type=jnp.float32)
            stage[0, head, picked] = (grad_q * scale).astype(jnp.bfloat16)

        for i, (acc, factor) in enumerate(((acc_k, scale), (acc_v, 1.0))):
            own[i, head] = acc[rows : 2 * rows] * factor
            part_out[0, i, head] = (acc[:rows] * factor).astype(jnp.bfloat16)
            part_out[1, i, head] = (acc[2 * rows :] * factor).astype(jnp.bfloat16)

    def send_parts(head):
        for i in range(2):
            for side in range(2):
                pltpu.make_async_remote_copy(
                    src_ref=part_out.at[side, i, head],
                    dst_ref=part_in.at[1 - side, i, head],
                    send_sem=part_send.at[i, side],
                    recv_sem=part_recv.at[i, 1 - side, head],
                    device_id=near[side],
                    device_id_type=MESH,
                ).start()

    def finish(head):
        for i, target in enumerate((dk_out, dv_out)):
            for side in range(2):
                wait_bytes(part_in.at[side, i, head], part_recv.at[i, side, head])
            total = (
                own[i, head]
                + part_in[0, i, head].astype(jnp.float32)
                + part_in[1, i, head].astype(jnp.float32)
            )
            stage[1 + i, head] = total.astype(jnp.bfloat16)
            send_result(1 + i, head, target)

    for head in range(AHEAD):
        send_inputs(pair_kv, head)

    lists.wait()
    tiles = lax.broadcasted_iota(jnp.int32, (3 * width, TILE), 0)
    first = (slab - 1) * width
    for t in range(width):
        hit = tiles < 0
        for n in range(listed.shape[1]):
            used = n < counts[slab * width + t]
            hit = hit | (tiles == jnp.where(used, listed[t, n] - first, -1))
        bias[:, t * TILE : (t + 1) * TILE] = jnp.where(hit, 0.0, -1e30)

    @pl.loop(0, head_count)
    def _(head):
        for i, window in enumerate((k_win, v_win)):
            wait_bytes(window.at[head, pl.ds(rows, rows)], in_recv.at[i, head])
        send_halo(head)

        @pl.when(head + AHEAD < head_count)
        def _():
            send_inputs(pair_kv, head + AHEAD)

        @pl.when(head + AHEAD >= head_count)
        def _():
            send_inputs(pair_qd, head + AHEAD - head_count)

    @pl.loop(0, head_count)
    def _(head):
        wait_bytes(q_rows.at[head], in_recv.at[2, head])
        wait_bytes(d_rows.at[head], in_recv.at[3, head])

        @pl.when(head + AHEAD < head_count)
        def _():
            send_inputs(pair_qd, head + AHEAD)

        for i, window in enumerate((k_win, v_win)):
            for side in range(2):
                wait_bytes(
                    window.at[head, pl.ds(2 * rows * side, rows)], halo_recv.at[i, side, head]
                )
        attend(head)
        send_parts(head)
        send_result(0, head, dq_out)

    @pl.loop(0, head_count)
    def _(head):
        finish(head)

    remote = pl.ds(0, rows - TILE)
    for i in range(4):
        wait_bytes(k_win.at[:, remote], in_send.at[i])
    for i in range(2):
        for side in range(2):
            wait_bytes(q_rows, halo_send.at[i, side])
            wait_bytes(q_rows, part_send.at[i, side])
    for i, target in enumerate((dq_out, dk_out, dv_out)):
        wait_bytes(stage.at[i, :, remote], out_send.at[i])
        wait_bytes(target, out_recv.at[i])


def per_device(slabs, width, queries, keys, values, grad_out, neighbours, counts):
    tile_rows, features = queries.shape
    head_count = features // DH // width
    rows = width * TILE
    block = min(512, rows)
    whole = pl.BlockSpec(memory_space=pl.ANY)
    half = jnp.bfloat16
    dma = pltpu.SemaphoreType.DMA
    flops = 5 * 2 * rows * 3 * rows * DH * head_count
    return pl.pallas_call(
        functools.partial(kernel, slabs, width, head_count, block),
        out_shape=[jax.ShapeDtypeStruct((tile_rows, features), half)] * 3,
        in_specs=[whole] * 5 + [pl.BlockSpec(memory_space=pltpu.SMEM)],
        out_specs=[whole] * 3,
        scratch_shapes=[
            pltpu.VMEM((head_count, rows, DH), half),
            pltpu.VMEM((head_count, rows, DH), half),
            pltpu.VMEM((head_count, 3 * rows, DH), half),
            pltpu.VMEM((head_count, 3 * rows, DH), half),
            pltpu.SMEM((width, neighbours.shape[1]), jnp.int32),
            pltpu.VMEM((3 * width, rows), jnp.float32),
            pltpu.VMEM((3 * rows, DH), jnp.float32),
            pltpu.VMEM((3 * rows, DH), jnp.float32),
            pltpu.VMEM((2, head_count, rows, DH), jnp.float32),
            pltpu.VMEM((2, 2, head_count, rows, DH), half),
            pltpu.VMEM((2, 2, head_count, rows, DH), half),
            pltpu.VMEM((3, head_count, rows, DH), half),
            dma(()),
            dma((4,)),
            dma((4, head_count)),
            dma((2, 2)),
            dma((2, 2, head_count)),
            dma((2, 2)),
            dma((2, 2, head_count)),
            dma((3,)),
            dma((3,)),
        ],
        compiler_params=pltpu.CompilerParams(
            collective_id=0, has_side_effects=True, vmem_limit_bytes=56 * 1024 * 1024
        ),
        cost_estimate=pl.CostEstimate(
            flops=flops, bytes_accessed=7 * tile_rows * features * 2, transcendentals=0
        ),
    )(queries, keys, values, grad_out, neighbours, counts)


def solution(mesh):
    split = P(("ctx", "head"), None)
    return jax.shard_map(
        functools.partial(per_device, mesh.shape["ctx"], mesh.shape["head"]),
        mesh=mesh,
        in_specs=(split, split, split, split, P(), P()),
        out_specs=(split, split, split),
        check_vma=False,
    )
```
